256 devices in a mesh: seq: 32 (over z_lo, x, core), uly: 8 (over y, z_hi).
Axes of the slice: x: 4, y: 4, z: 8 (z_hi: 2, z_lo: 4; z = z_hi * 4 + z_lo), core: 2. Of those that a mesh axis runs over, the one named last changes fastest.
Arguments:
- tokens: bfloat16 [16384, 3072], P(('seq', 'uly')), may hold values from -6 to 6
- mod_shift: float32 [3072], replicated, may hold values from -3 to 3
- mod_scale: float32 [3072], replicated, may hold values from -0.5 to 0.5
- mod_gate: float32 [3072], replicated, may hold values from 0.5 to 2
- w_query: bfloat16 [3072, 2048], P(None, 'uly'), may hold values from -0.109375 to 0.109375
- w_key: bfloat16 [3072, 2048], P(None, 'uly'), may hold values from -0.109375 to 0.109375
- w_value: bfloat16 [3072, 2048], P(None, 'uly'), may hold values from -0.109375 to 0.109375
- q_gain: float32 [128], replicated, may hold values from 0.5 to 10
- k_gain: float32 [128], replicated, may hold values from 0.5 to 10
- w_out: bfloat16 [2048, 3072], P('uly'), may hold values from -0.125 to 0.125
- kv_blocks: int32 [128, 50], P('seq'), may hold values from 0 to 127, as said below
- kv_count: int32 [128], P('seq'), may hold values from 8 to 50
Outputs:
- branch_out: bfloat16 [16384, 3072], P(('seq', 'uly'))
The draws below stay inside these ranges and needn't reach their ends.
Inputs may be any that keep to these rules, and one draw needn't show every extreme that they name: `kv_blocks`: each row names distinct key blocks. The attended set of a query block always holds every block of its own frame and of the frames beside it. From any one frame at distance two or more, the attended sets of all query blocks of one frame together hold at most 2 blocks; entries past kv_count are other blocks and are ignored.
All inputs are finite; a program needn't handle non-finite values.
Results may differ from the reference program's by a relative error of at most 0.025.
The reference program's roundings to bfloat16 on the way count: a program that leaves them out, or rounds other values in their place, can miss the bound.
Values may be sent and summed in bfloat16 or wider, within the bound.
A program may use at most 192 MiB of HBM per device.

```python
import jax
import jax.numpy as jnp
from jax import lax

D = 3072
HEAD_DIM = 128
HEADS = 16
BLK = 128
FB = 4
CAP = 2
KMAX = 50
TOKENS = 16384
N_BLOCKS = 128
N_SEQ = 32


def radial_lists(key):
    block_ids = jnp.arange(N_BLOCKS, dtype=jnp.int32)
    query_frame = block_ids // FB
    key_frame = block_ids // FB
    within = block_ids % FB
    distance = jnp.abs(query_frame[:, None] - key_frame[None, :])
    frame_ids = jnp.arange(N_SEQ, dtype=jnp.int32)
    frame_gap = jnp.abs(frame_ids[:, None] - frame_ids[None, :])
    frame_draws = jax.random.randint(jax.random.fold_in(key, 13), (N_SEQ, N_SEQ), 0, 2 ** 20) * N_SEQ + frame_ids[None, :]
    frame_scores = jnp.where(frame_gap >= 3, frame_draws, 2 ** 30)
    frame_rank = jnp.argsort(jnp.argsort(frame_scores, axis=1), axis=1).astype(jnp.int32)
    doubled = frame_rank < (N_SEQ - 1) // 4
    pair_doubled = doubled[query_frame[:, None], key_frame[None, :]]
    draws = jax.random.randint(jax.random.fold_in(key, 11), (N_SEQ, N_SEQ, FB), 0, 2 ** 20)
    scored = draws * FB + jnp.arange(FB, dtype=jnp.int32)[None, None, :]
    ranking = jnp.argsort(jnp.argsort(scored, axis=-1), axis=-1).astype(jnp.int32)
    pair_rank = ranking[query_frame[:, None], key_frame[None, :], within[None, :]]
    quota = jnp.where((distance == 2) | pair_doubled, CAP, 1)
    chosen = (distance <= 1) | (pair_rank < quota)
    coins = jax.random.randint(jax.random.fold_in(key, 12), (N_BLOCKS, N_BLOCKS), 0, 4) < 3
    keeper = (distance <= 1) | (within[:, None] == 0) | coins
    include = chosen & keeper
    counts = jnp.sum(include.astype(jnp.int32), axis=1)
    ordering = jnp.where(include, 0, 1) * N_BLOCKS + block_ids[None, :]
    lists = jnp.argsort(ordering, axis=1)[:, :KMAX]
    return (lists.astype(jnp.int32), counts.astype(jnp.int32))


def spread_gain(key, top):
    level = jax.random.uniform(key, (HEAD_DIM,), jnp.float32, jnp.log(0.5), jnp.log(top))
    return jnp.exp(level)


def draw_kv_blocks(key, part):
    lists, counts = radial_lists(key)
    return lists


def draw_kv_count(key, part):
    lists, counts = radial_lists(key)
    return counts


def draw_q_gain(key, part):
    key = jax.random.fold_in(key, 1)
    return spread_gain(key, 4.0)


def draw_k_gain(key, part):
    key = jax.random.fold_in(key, 2)
    return spread_gain(key, 4.0)


def shard_levels(key, dims, pieces, least, top_value):
    def one(axis_at, shards_of):
        steps = jax.random.uniform(jax.random.fold_in(jax.random.fold_in(key, 6), axis_at), (shards_of,), jnp.float32, least / len(pieces), top_value / len(pieces))
        return jnp.repeat(jnp.exp(steps), dims[axis_at] // shards_of).reshape((-1,) + (1,) * (len(dims) - axis_at - 1))

    level = one(*pieces[0])
    for cut in pieces[1:]:
        level = level * one(*cut)
    return level


def normal_values(rng, extent, deviation, bound, shards=(), kind=jnp.bfloat16):
    result = jax.random.normal(rng, extent, jnp.float32) * deviation
    if len(shards) > 0:
        result = shard_levels(rng, extent, shards, -0.22, 0.18) * result
    return jnp.clip(result, min=-bound, max=bound).astype(kind)


def setup_inputs(seed: int = 0) -> dict:
    streams_of = jax.random.split(jax.random.key(seed), 13)
    return {
        "tokens": normal_values(streams_of[0], (TOKENS, D), 1.0, 6.0, ((0, 256),)),
        "mod_shift": normal_values(streams_of[1], (D,), 0.5, 3.0, (), jnp.float32),
        "mod_scale": jnp.clip(jax.random.uniform(streams_of[2], (D,), jnp.float32, -0.5, 0.5), -0.5, 0.5),
        "mod_gate": jnp.clip(jax.random.uniform(streams_of[3], (D,), jnp.float32, 0.5, 2.0), 0.5, 2.0),
        "w_query": normal_values(streams_of[4], (D, HEADS * HEAD_DIM), D ** -0.5, 0.109375, ((1, 8),)),
        "w_key": normal_values(streams_of[5], (D, HEADS * HEAD_DIM), D ** -0.5, 0.109375, ((1, 8),)),
        "w_value": normal_values(streams_of[6], (D, HEADS * HEAD_DIM), D ** -0.5, 0.109375, ((1, 8),)),
        "q_gain": draw_q_gain(jax.random.fold_in(streams_of[12], 71), 0),
        "k_gain": draw_k_gain(jax.random.fold_in(streams_of[12], 71), 0),
        "w_out": normal_values(streams_of[9], (HEADS * HEAD_DIM, D), (HEADS * HEAD_DIM) ** -0.5, 0.125, ((0, 8),)),
        "kv_blocks": draw_kv_blocks(jax.random.fold_in(streams_of[12], 71), 0),
        "kv_count": draw_kv_count(jax.random.fold_in(streams_of[12], 71), 0),
    }


eps = 1e-06

def modulate(tokens, mod_shift, mod_scale):
    values = tokens.astype(jnp.float32)
    center = lax.optimization_barrier(jnp.mean(values, axis=-1, keepdims=True))
    spread = lax.optimization_barrier(jnp.mean(jnp.square(values - center), axis=-1, keepdims=True))
    normed = (values - center) * lax.rsqrt(spread + eps)
    return (normed * (1.0 + mod_scale) + mod_shift).astype(jnp.bfloat16)

def head_norm(projected, gain, heads):
    shaped = projected.reshape(projected.shape[0], heads, gain.shape[0])
    power = lax.optimization_barrier(jnp.mean(jnp.square(shaped), axis=-1, keepdims=True))
    return (shaped * lax.rsqrt(power + eps) * gain).astype(jnp.bfloat16)

def reference(tokens, mod_shift, mod_scale, mod_gate, w_query, w_key, w_value, q_gain, k_gain, w_out, kv_blocks, kv_count):
    modded = modulate(tokens, mod_shift, mod_scale)
    queries = head_norm(jnp.dot(modded, w_query, preferred_element_type=jnp.float32), q_gain, HEADS)
    keys = head_norm(jnp.dot(modded, w_key, preferred_element_type=jnp.float32), k_gain, HEADS)
    values = jnp.dot(modded, w_value, preferred_element_type=jnp.float32).astype(jnp.bfloat16)
    values = values.reshape(TOKENS, HEADS, HEAD_DIM)
    key_blocks = keys.reshape(N_BLOCKS, BLK, HEADS, HEAD_DIM)
    value_blocks = values.reshape(N_BLOCKS, BLK, HEADS, HEAD_DIM)
    scale = HEAD_DIM ** (-0.5)

    def attend(index):
        listed = kv_blocks[index]
        valid = jnp.arange(KMAX, dtype=jnp.int32) < kv_count[index]
        chosen_keys = key_blocks[listed].reshape(KMAX * BLK, HEADS, HEAD_DIM).astype(jnp.float32)
        chosen_values = value_blocks[listed].reshape(KMAX * BLK, HEADS, HEAD_DIM).astype(jnp.float32)
        block_queries = lax.dynamic_slice_in_dim(queries, index * BLK, BLK, 0).astype(jnp.float32)
        scores = jnp.einsum('qhd,khd->hqk', block_queries, chosen_keys) * scale
        mask = jnp.repeat(valid, BLK)[None, None, :]
        scores = jnp.where(mask, scores, -1e+30)
        peak = lax.optimization_barrier(jnp.max(scores, axis=-1, keepdims=True))
        weights = jnp.where(mask, jnp.exp(scores - peak), 0.0)
        norm_sum = lax.optimization_barrier(jnp.sum(weights, axis=-1))
        rounded = lax.optimization_barrier(weights.astype(jnp.bfloat16)).astype(jnp.float32)
        mixed = jnp.einsum('hqk,khd->qhd', rounded, chosen_values) / jnp.transpose(norm_sum)[:, :, None]
        return mixed.astype(jnp.bfloat16)
    attended = lax.map(attend, jnp.arange(N_BLOCKS, dtype=jnp.int32)).reshape(TOKENS, HEADS * HEAD_DIM)
    projected = jnp.dot(attended, w_out, preferred_element_type=jnp.float32)
    return (projected * mod_gate).astype(jnp.bfloat16)
```

```python
import functools
import math

import jax
import jax.numpy as jnp
from jax import lax
from jax.experimental import pallas as pl
from jax.experimental.pallas import tpu as pltpu
from jax.sharding import PartitionSpec as P

MESH = pl.DeviceIdType.MESH
EPS = 1e-06
D = 3072
HD = 128
LOW = -1e30
CC = D // 2


def pick(cond, a, b):
    return jnp.where(cond, a, b)


def kernel(
    tokens_ref, shift_ref, scale_ref, gate_ref, wq_ref, wk_ref, wv_ref, qg_ref, kg_ref, wo_ref, lists_ref,
    out_ref,
    w, wo, tok, lst, tabv, tabs, stage, qbuf, kv, kvp, m, l, o, attb, atts, part, rfwd, ra, rb, rz, zsend,
    wsem, lsem, tsend, trecv, ssend, srecv, ksend, krecv, asend, arecv, rsend, rrecv,
):
    s = lax.axis_index("seq")
    u = lax.axis_index("uly")
    zl, x, c = s // 8, (s // 2) % 4, s % 2
    i, p = zl % 2, zl // 2
    y, zh = u // 2, u % 2
    d = 1 - 2 * c

    def xdev(e):
        return (zl * 8 + ((x + e + 8) % 4) * 2 + c, u)

    def yy(e):
        return (y + e + 8) % 4

    def ydev(e):
        return (s, yy(e) * 2 + zh)

    core_dev = (s + 1 - 2 * c, u)
    pair_dev = (s + 8 * (1 - 2 * i), u)
    far_dev = (s + 16 * (1 - 2 * p), u)
    anti_dev = (s, y * 2 + 1 - zh)

    def rcopy(src, dst, ss, rs, dev):
        return pltpu.make_async_remote_copy(
            src_ref=src, dst_ref=dst, send_sem=ss, recv_sem=rs, device_id=dev, device_id_type=MESH
        )

    wcopies = [pltpu.make_async_copy(r, w.at[n], wsem.at[n]) for n, r in enumerate((wq_ref, wk_ref, wv_ref))]
    wcopies.append(pltpu.make_async_copy(wo_ref, wo, wsem.at[3]))
    for cp in wcopies:
        cp.start()

    barrier = pltpu.get_barrier_semaphore()
    for dev in (core_dev, pair_dev, far_dev, anti_dev, xdev(1), xdev(-1), ydev(1), ydev(-1)):
        pl.semaphore_signal(barrier, inc=1, device_id=dev, device_id_type=MESH)

    vals = tokens_ref[...].astype(jnp.float32)
    center = jnp.mean(vals, axis=-1, keepdims=True)
    vals = vals - center
    spread = jnp.mean(vals * vals, axis=-1, keepdims=True)
    vals = vals * lax.rsqrt(spread + EPS)
    tok[0, y] = (vals * (1.0 + scale_ref[...]) + shift_ref[...]).astype(jnp.bfloat16)
    lst[i] = lists_ref[...]

    pl.semaphore_wait(barrier, 8)

    def half_rows(n):
        return pl.ds(32 * n, 32)

    def t_anti(n):
        return rcopy(tok.at[0, y, half_rows(n)], tok.at[1, y, half_rows(n)], tsend.at[n], trecv.at[n], anti_dev)

    def t_own(e):
        k = 2 if e == 1 else 3
        return rcopy(tok.at[0, y], tok.at[0, y], tsend.at[k], trecv.at[k], ydev(d * e))

    def t_own_in(e):
        k = 2 if e == 1 else 3
        sl = yy(-d * e)
        return rcopy(tok.at[0, sl], tok.at[0, sl], tsend.at[k], trecv.at[k], ydev(d * e))

    def t_fwd():
        sl = yy(-d)
        return rcopy(tok.at[0, sl], tok.at[0, sl], tsend.at[4], trecv.at[4], ydev(d))

    def t_fwd_in():
        sl = yy(2)
        return rcopy(tok.at[0, sl], tok.at[0, sl], tsend.at[4], trecv.at[4], ydev(d))

    def t_other(n, e, sl):
        k = 5 + 2 * n + (0 if e == 1 else 1)
        return rcopy(tok.at[1, sl, half_rows(n)], tok.at[1, sl, half_rows(n)], tsend.at[k], trecv.at[k], ydev(d * e))

    def t_other_fwd(n, sl):
        k = 9 + n
        return rcopy(tok.at[1, sl, half_rows(n)], tok.at[1, sl, half_rows(n)], tsend.at[k], trecv.at[k], ydev(d))

    def l_copy(row):
        return rcopy(lst.at[row], lst.at[row], lsem.at[0], lsem.at[1], pair_dev)

    l_copy(i).start()
    t_anti(0).start()
    t_own(1).start()
    t_own(-1).start()
    t_anti(1).start()

    m[...] = jnp.full(m.shape, LOW, jnp.float32)
    l[...] = jnp.zeros(l.shape, jnp.float32)
    o[...] = jnp.zeros(o.shape, jnp.float32)
    l_copy(1 - i).wait_recv()
    first, second = lst[0], lst[1]
    listed = jnp.concatenate([first[0:4], second[0:4]], axis=0)
    counts = jnp.concatenate([first[4:8], second[4:8]], axis=0)
    lane = lax.broadcasted_iota(jnp.int32, (8, 128), 1)
    row = lax.broadcasted_iota(jnp.int32, (8, 128), 0)
    listed = jnp.where(lane < counts, listed, -1)
    member = jnp.zeros((8, 128), jnp.int32)
    for e in range(50):
        member = jnp.where(listed[:, e : e + 1] == lane, 1, member)
    union = jnp.where(
        row < 4,
        jnp.max(member[0:4], axis=0, keepdims=True),
        jnp.max(member[4:8], axis=0, keepdims=True),
    )

    def ahead(a, n):
        return a if n == 0 else pltpu.roll(a, 128 - n, 1)

    us = [ahead(union, n) > 0 for n in range(4)]
    ms = [ahead(member, n) for n in range(4)]
    f0 = 2 * p * 8 + x * 2 + c
    near = jnp.abs((lane >> 2) - jnp.where(row < 4, f0, f0 + 8)) <= 1
    idx0 = jnp.where(us[0], 0, jnp.where(us[1], 1, jnp.where(us[2], 2, 3)))
    idx1 = jnp.where(us[3], 3, jnp.where(us[2], 2, jnp.where(us[1], 1, 0)))
    idx1 = jnp.where(idx1 == idx0, (idx0 + 1) & 3, idx1)
    idx0 = jnp.where(near, 0, idx0)
    idx1 = jnp.where(near, 1, idx1)

    def at(idx):
        return jnp.where(idx == 0, ms[0], jnp.where(idx == 1, ms[1], jnp.where(idx == 2, ms[2], ms[3])))

    tabv[0] = idx0
    tabv[1] = idx1
    tabv[2] = at(idx0)
    tabv[3] = at(idx1)
    tcopy = pltpu.make_async_copy(tabv, tabs, wsem.at[4])
    tcopy.start()
    tcopy.wait()
    l_copy(i).wait_send()

    for cp in wcopies[:3]:
        cp.wait()

    slot_own = p * 8 + x * 2 + c

    def project(h):
        a = tok[h].reshape(256, D)
        for n, gain in enumerate((qg_ref, kg_ref, None)):
            acc = jnp.dot(a, w[n], preferred_element_type=jnp.float32)
            for hd in range(2):
                piece = acc[:, hd * HD : (hd + 1) * HD]
                if gain is not None:
                    power = jnp.mean(piece * piece, axis=-1, keepdims=True)
                    piece = piece * lax.rsqrt(power + EPS) * gain[...]
                stage[h, hd, n] = piece.astype(jnp.bfloat16)

    def s_kv(h, who):
        return rcopy(stage.at[h, 1 - i, pl.ds(1, 2)], kv.at[slot_own, h, who], ssend.at[h, 0], srecv.at[h, 0], pair_dev)

    def s_q(h, who):
        return rcopy(stage.at[h, 1 - i, 0], qbuf.at[who, h], ssend.at[h, 1], srecv.at[h, 1], pair_dev)

    def swap_out(h):
        s_kv(h, i).start()
        s_q(h, i).start()
        kv[slot_own, h, i] = stage[h, i, 1:3]
        qbuf[i, h] = stage[h, i, 0]

    def k_copy(h, slot, e, dev):
        return rcopy(kv.at[slot, h], kv.at[slot, h], ksend.at[h, e], krecv.at[h, slot], dev)

    def swap_in(h):
        s_kv(h, 1 - i).wait_recv()
        k_copy(h, slot_own, 0, far_dev).start()
        k_copy(h, slot_own, 1, xdev(1)).start()
        k_copy(h, slot_own, 2, xdev(-1)).start()
        k_copy(h, slot_own, 3, core_dev).start()
        s_q(h, 1 - i).wait_recv()

    t_own_in(1).wait_recv()
    t_fwd().start()
    t_anti(0).wait_recv()
    t_other(0, 1, y).start()
    t_other(0, -1, y).start()
    t_own_in(-1).wait_recv()
    t_fwd_in().wait_recv()
    project(0)
    swap_out(0)
    t_anti(1).wait_recv()
    t_other(1, 1, y).start()
    t_other(1, -1, y).start()
    t_other(0, 1, yy(-d)).wait_recv()
    t_other_fwd(0, yy(-d)).start()
    swap_in(0)

    factor = (HD ** -0.5) * math.log2(math.e)
    lane1 = lax.broadcasted_iota(jnp.int32, (1, 128), 1)

    def attend(fi, h, parts):
        q = qbuf[fi, h]
        old = m[fi, h]
        new = old
        tiles = []
        for keys, _, bias in parts:
            scores = lax.dot_general(q, keys, (((1,), (1,)), ((), ())), preferred_element_type=jnp.float32) * factor
            if bias is not None:
                scores = (scores.reshape(4, 64, 256) + bias).reshape(256, 256)
            tiles.append(scores)
            new = jnp.maximum(new, jnp.max(scores, axis=1, keepdims=True))
        decay = jnp.exp2(old - new)
        total = l[fi, h] * decay
        summed = o[fi, h] * decay
        for scores, (_, values, _) in zip(tiles, parts):
            left = jnp.exp2(scores[:, :128] - new)
            right = jnp.exp2(scores[:, 128:] - new)
            total = total + (left + right)
            weights = jnp.concatenate([left.astype(jnp.bfloat16), right.astype(jnp.bfloat16)], axis=1)
            summed = summed + jnp.dot(weights, values, preferred_element_type=jnp.float32)
        m[fi, h] = new
        l[fi, h] = total
        o[fi, h] = summed

    def near_pass(n, carry):
        fi, df = n // 3, n % 3 - 1
        f = (2 * p + fi) * 8 + x * 2 + c + df

        @pl.when(jnp.logical_and(f >= 0, f <= 31))
        def _():
            fz = f // 8
            slot = (fz // 2) * 8 + f % 8
            keys = jnp.concatenate([kv[slot, h, fz % 2, 0, 128:256] for h in range(2)], axis=0)
            values = jnp.concatenate([kv[slot, h, fz % 2, 1, 128:256] for h in range(2)], axis=0)
            for h in range(2):
                attend(fi, h, [(keys, values, None)])

        return carry

    def chosen(fi, base):
        rows, bias = [], []
        for ff in range(2):
            at4 = (base + 8 * ff) * 4
            rows.append([tabs[t, fi * 4, at4] for t in range(2)])
            rowsb = []
            for b in range(4):
                b0 = jnp.where(tabs[2, fi * 4 + b, at4] > 0, 0.0, LOW)
                b1 = jnp.where(tabs[3, fi * 4 + b, at4] > 0, 0.0, LOW)
                rowsb.append(jnp.where(lane1 < 64, b0, b1).reshape(1, 1, 128))
            bias.append(jnp.concatenate(rowsb, axis=0))
        bias = jnp.concatenate(bias, axis=2)

        def group(kh):
            return tuple(
                jnp.concatenate([kvp[kh, ff, t, rows[ff][e]] for ff in range(2) for e in range(2)], axis=0)
                for t in range(2)
            ) + (bias,)

        return group

    def step(h, k, carry):
        j, oc = k // 2, k % 2

        if h == 0:

            @pl.when(k == 2)
            def _():
                t_other(1, 1, yy(-d)).wait_recv()
                t_other_fwd(1, yy(-d)).start()

            @pl.when(k == 4)
            def _():
                for e in range(2):
                    t_other(e, -1, yy(d)).wait_recv()
                    t_other_fwd(e, yy(2)).wait_recv()
                project(1)
                swap_out(1)

            @pl.when(k == 8)
            def _():
                swap_in(1)

        else:

            @pl.when(k == 14)
            def _():
                lax.fori_loop(0, 6, near_pass, 0)

        dp = pick(j == 3, 1, pick(j >= 5, 1, 0))
        dxs = pick(j % 4 == 1, -1, pick(j == 2, 1, pick(j == 6, 1, pick(j == 4, 2, pick(j == 7, 2, 0)))))
        dd = d * (1 - 2 * oc)
        slot = ((p + dp) % 2) * 8 + ((x + dd * dxs + 8) % 4) * 2 + (c + oc) % 2

        @pl.when(k > 0)
        def _():
            k_copy(h, slot, 0, core_dev).wait_recv()

        @pl.when(jnp.logical_and(oc == 0, j > 0))
        def _():
            k_copy(h, slot, 3 + j, core_dev).start()

        @pl.when(jnp.logical_and(oc == 0, j % 4 == 1))
        def _():
            k_copy(h, slot, 11 + j // 4, xdev(d)).start()

        @pl.when(jnp.logical_and(oc == 0, j == 3))
        def _():
            k_copy(h, slot, 13, xdev(1)).start()
            k_copy(h, slot, 14, xdev(-1)).start()

        for kh in range(h + 1):
            kvp[kh] = kv[slot, kh].reshape(2, 2, 4, 64, HD)
        base = (slot // 8) * 16 + slot % 8
        for fi in range(2):
            group = chosen(fi, base)
            late = group(h)
            attend(fi, 0, [late])
            if h == 1:
                attend(fi, 1, [group(0), late])
        return carry

    lax.fori_loop(0, 16, functools.partial(step, 0), 0)
    lax.fori_loop(0, 16, functools.partial(step, 1), 0)

    def result(fi, h):
        total = jnp.sum(l[fi, h], axis=1, keepdims=True)
        return (o[fi, h] / total).astype(jnp.bfloat16)

    def a_copy(h, head):
        return rcopy(atts.at[h], attb.at[head, h], asend.at[h], arecv.at[h], pair_dev)

    for h in (1, 0):
        atts[h] = result(1 - i, h)
        a_copy(h, i).start()
    for h in (1, 0):
        attb[i, h] = result(i, h)
    wcopies[3].wait()

    def r_out(q, dest):
        return rcopy(part.at[q, dest], rfwd.at[q], rsend.at[q, 0], rrecv.at[q, 0], ydev(d))

    def r_a(q):
        return rcopy(part.at[q, yy(d)], ra.at[q], rsend.at[q, 1], rrecv.at[q, 1], ydev(d))

    def r_b(q):
        return rcopy(part.at[q, yy(-d)], rb.at[q], rsend.at[q, 2], rrecv.at[q, 2], ydev(-d))

    def r_z(cc):
        return rcopy(zsend.at[cc], rz.at[cc], rsend.at[2 + cc, 3], rrecv.at[2 + cc, 3], anti_dev)

    for h in (1, 0):
        a_copy(h, 1 - i).wait_recv()
        rows = jnp.concatenate([attb[0, h], attb[1, h]], axis=1)
        for cc in range(2):
            q = 2 * h + cc

            def cols(t, carry):
                at_col = pl.multiple_of(cc * CC + t * 256, 256)
                res = jnp.dot(rows, wo[:, pl.ds(at_col, 256)], preferred_element_type=jnp.float32)
                part[q, :, :, pl.ds(pl.multiple_of(t * 256, 256), 256)] = res.astype(jnp.bfloat16).reshape(4, 64, 256)
                return carry

            lax.fori_loop(0, CC // 256, cols, 0)
            r_out(q, yy(2)).start()
            r_b(q).start()

    def chain(q):
        r_out(q, yy(2)).wait_recv()
        part[q, yy(d)] = (part[q, yy(d)].astype(jnp.float32) + rfwd[q].astype(jnp.float32)).astype(jnp.bfloat16)
        r_a(q).start()

    def gathered(q):
        r_a(q).wait_recv()
        r_b(q).wait_recv()
        return part[q, y].astype(jnp.float32) + ra[q].astype(jnp.float32) + rb[q].astype(jnp.float32)

    def to_anti(cc):
        zsend[cc] = gathered(2 + cc).astype(jnp.bfloat16)
        r_z(cc).start()

    def finish(cc):
        total = gathered(cc)
        r_z(cc).wait_recv()
        cols = slice(cc * CC, (cc + 1) * CC)
        out_ref[:, cols] = ((total + rz[cc].astype(jnp.float32)) * gate_ref[:, cols]).astype(jnp.bfloat16)

    chain(2)
    chain(3)
    to_anti(0)
    chain(0)
    to_anti(1)
    chain(1)
    finish(0)
    finish(1)

    for n in range(2):
        t_anti(n).wait_send()
        t_other(n, 1, y).wait_send()
        t_other(n, -1, y).wait_send()
        t_other_fwd(n, yy(-d)).wait_send()
    t_own(1).wait_send()
    t_own(-1).wait_send()
    t_fwd().wait_send()
    for h in range(2):
        s_kv(h, i).wait_send()
        s_q(h, i).wait_send()
        a_copy(h, i).wait_send()
        for e in range(15):
            k_copy(h, slot_own, e, core_dev).wait_send()
    for q in range(4):
        r_out(q, yy(2)).wait_send()
        r_a(q).wait_send()
        r_b(q).wait_send()
    for cc in range(2):
        r_z(cc).wait_send()


def body(tokens, mod_shift, mod_scale, mod_gate, w_query, w_key, w_value, q_gain, k_gain, w_out, kv_blocks, kv_count):
    lists = jnp.concatenate(
        [jnp.pad(kv_blocks, ((0, 0), (0, 78))), jnp.broadcast_to(kv_count[:, None], (4, 128))], axis=0
    )
    vmem = pl.BlockSpec(memory_space=pltpu.VMEM)
    hbm = pl.BlockSpec(memory_space=pl.ANY)
    bf16, f32 = jnp.bfloat16, jnp.float32
    dma = pltpu.SemaphoreType.DMA
    return pl.pallas_call(
        kernel,
        out_shape=jax.ShapeDtypeStruct((64, D), bf16),
        in_specs=[vmem, vmem, vmem, vmem, hbm, hbm, hbm, vmem, vmem, hbm, vmem],
        out_specs=vmem,
        scratch_shapes=[
            pltpu.VMEM((3, D, 256), bf16),
            pltpu.VMEM((256, D), bf16),
            pltpu.VMEM((2, 4, 64, D), bf16),
            pltpu.VMEM((2, 8, 128), jnp.int32),
            pltpu.VMEM((4, 8, 128), jnp.int32),
            pltpu.SMEM((4, 8, 128), jnp.int32),
            pltpu.VMEM((2, 2, 3, 256, HD), bf16),
            pltpu.VMEM((2, 2, 256, HD), bf16),
            pltpu.VMEM((16, 2, 2, 2, 256, HD), bf16),
            pltpu.VMEM((2, 2, 2, 4, 64, HD), bf16),
            pltpu.VMEM((2, 2, 256, 128), f32),
            pltpu.VMEM((2, 2, 256, 128), f32),
            pltpu.VMEM((2, 2, 256, HD), f32),
            pltpu.VMEM((2, 2, 256, HD), bf16),
            pltpu.VMEM((2, 256, HD), bf16),
            pltpu.VMEM((4, 4, 64, CC), bf16),
            pltpu.VMEM((4, 64, CC), bf16),
            pltpu.VMEM((4, 64, CC), bf16),
            pltpu.VMEM((4, 64, CC), bf16),
            pltpu.VMEM((2, 64, CC), bf16),
            pltpu.VMEM((2, 64, CC), bf16),
            dma((5,)),
            dma((2,)),
            dma((11,)),
            dma((11,)),
            dma((2, 2)),
            dma((2, 2)),
            dma((2, 15)),
            dma((2, 16)),
            dma((2,)),
            dma((2,)),
            dma((4, 4)),
            dma((4, 4)),
        ],
        compiler_params=pltpu.CompilerParams(
            collective_id=0, has_side_effects=True, vmem_limit_bytes=48 * 2**20
        ),
        name="radial_block",
    )(
        tokens,
        mod_shift.reshape(1, D),
        mod_scale.reshape(1, D),
        mod_gate.reshape(1, D),
        w_query,
        w_key,
        w_value,
        q_gain.reshape(1, HD),
        k_gain.reshape(1, HD),
        w_out,
        lists,
    )


def solution(mesh):
    placed = (
        P(("seq", "uly"), None),
        P(),
        P(),
        P(),
        P(None, "uly"),
        P(None, "uly"),
        P(None, "uly"),
        P(),
        P(),
        P("uly", None),
        P("seq", None),
        P("seq"),
    )
    return jax.shard_map(
        body, mesh=mesh, in_specs=placed, out_specs=P(("seq", "uly"), None), check_vma=False
    )
```

```python
import functools
import math

import jax
import jax.numpy as jnp
from jax import lax
from jax.experimental import pallas as pl
from jax.experimental.pallas import tpu as pltpu
from jax.sharding import PartitionSpec as P

MESH = pl.DeviceIdType.MESH
EPS = 1e-06
D = 3072
HD = 128
LOW = -1e30
NC = 4
CW = D // NC


def pick(cond, a, b):
    return jnp.where(cond, a, b)


def kernel(
    tokens_in, shift_in, scale_in, gate_in, wq_ref, wk_ref, wv_ref, qg_in, kg_in, wo_ref, lists_in, counts_in,
    out_ref,
    tokens_ref, shift_ref, scale_ref, gate_ref, qg_ref, kg_ref,
    w, wo, tok, lst, cnt, tabv, tabs, stq, stkv, qbuf, kv, kvp, m, l, o, attb, atts, part, rfwd, ra, rb, rz, zsend,
    isem, wsem, lsem, tsend, trecv, ssend, srecv, ksend, krecv, asend, arecv, rsend, rrecv,
):
    s = lax.axis_index("seq")
    u = lax.axis_index("uly")
    zl, x, c = s // 8, (s // 2) % 4, s % 2
    i, p = zl % 2, zl // 2
    y, zh = u // 2, u % 2
    d = 1 - 2 * c

    def xdev(e):
        return (zl * 8 + ((x + e + 8) % 4) * 2 + c, u)

    def yy(e):
        return (y + e + 8) % 4

    def ydev(e):
        return (s, yy(e) * 2 + zh)

    core_dev = (s + 1 - 2 * c, u)
    pair_dev = (s + 8 * (1 - 2 * i), u)
    far_dev = (s + 16 * (1 - 2 * p), u)
    anti_dev = (s, y * 2 + 1 - zh)

    def rcopy(src, dst, ss, rs, dev):
        return pltpu.make_async_remote_copy(
            src_ref=src, dst_ref=dst, send_sem=ss, recv_sem=rs, device_id=dev, device_id_type=MESH
        )

    icopies = [
        pltpu.make_async_copy(src, dst, isem.at[n])
        for n, (src, dst) in enumerate(
            (
                (tokens_in, tokens_ref),
                (scale_in, scale_ref),
                (shift_in, shift_ref),
                (lists_in, lst.at[i]),
                (counts_in, cnt.at[i]),
                (qg_in, qg_ref),
                (kg_in, kg_ref),
                (gate_in, gate_ref),
            )
        )
    ]
    wcopies = [pltpu.make_async_copy(r, w.at[n], wsem.at[n]) for n, r in enumerate((wq_ref, wk_ref, wv_ref))]
    wcopies.append(pltpu.make_async_copy(wo_ref, wo, wsem.at[3]))
    for cp in icopies + wcopies:
        cp.start()

    barrier = pltpu.get_barrier_semaphore()
    for dev in (core_dev, pair_dev, far_dev, anti_dev, xdev(1), xdev(-1), ydev(1), ydev(-1)):
        pl.semaphore_signal(barrier, inc=1, device_id=dev, device_id_type=MESH)

    for cp in icopies:
        cp.wait()
    vals = tokens_ref[...].astype(jnp.float32)
    center = jnp.mean(vals, axis=-1, keepdims=True)
    vals = vals - center
    spread = jnp.mean(vals * vals, axis=-1, keepdims=True)
    vals = vals * lax.rsqrt(spread + EPS)
    tok[0, y] = (vals * (1.0 + scale_ref[...]) + shift_ref[...]).astype(jnp.bfloat16)

    pl.semaphore_wait(barrier, 8)

    def half_rows(n):
        return pl.ds(32 * n, 32)

    def t_anti(n):
        return rcopy(tok.at[0, y, half_rows(n)], tok.at[1, y, half_rows(n)], tsend.at[n], trecv.at[n], anti_dev)

    def t_own(e):
        k = 2 if e == 1 else 3
        return rcopy(tok.at[0, y], tok.at[0, y], tsend.at[k], trecv.at[k], ydev(d * e))

    def t_own_in(e):
        k = 2 if e == 1 else 3
        sl = yy(-d * e)
        return rcopy(tok.at[0, sl], tok.at[0, sl], tsend.at[k], trecv.at[k], ydev(d * e))

    def t_fwd():
        sl = yy(-d)
        return rcopy(tok.at[0, sl], tok.at[0, sl], tsend.at[4], trecv.at[4], ydev(d))

    def t_fwd_in():
        sl = yy(2)
        return rcopy(tok.at[0, sl], tok.at[0, sl], tsend.at[4], trecv.at[4], ydev(d))

    def t_other(n, e, sl):
        k = 5 + 2 * n + (0 if e == 1 else 1)
        return rcopy(tok.at[1, sl, half_rows(n)], tok.at[1, sl, half_rows(n)], tsend.at[k], trecv.at[k], ydev(d * e))

    def t_other_fwd(n, sl):
        k = 9 + n
        return rcopy(tok.at[1, sl, half_rows(n)], tok.at[1, sl, half_rows(n)], tsend.at[k], trecv.at[k], ydev(d))

    def l_copy(row):
        return rcopy(lst.at[row], lst.at[row], lsem.at[0], lsem.at[1], pair_dev)

    def c_copy(row):
        return rcopy(cnt.at[row], cnt.at[row], lsem.at[2], lsem.at[3], pair_dev)

    l_copy(i).start()
    c_copy(i).start()
    t_anti(0).start()
    t_own(1).start()
    t_own(-1).start()
    t_anti(1).start()

    m[...] = jnp.full(m.shape, LOW, jnp.float32)
    l[...] = jnp.zeros(l.shape, jnp.float32)
    o[...] = jnp.zeros(o.shape, jnp.float32)
    l_copy(1 - i).wait_recv()
    c_copy(1 - i).wait_recv()
    listed = jnp.concatenate([lst[0], lst[1]], axis=0)
    lane = lax.broadcasted_iota(jnp.int32, (8, 128), 1)
    row = lax.broadcasted_iota(jnp.int32, (8, 128), 0)
    counts = jnp.zeros((8, 128), jnp.int32)
    for e in range(8):
        counts = jnp.where(row == e, cnt[e // 4][:, e % 4 : e % 4 + 1], counts)
    member = jnp.zeros((8, 128), jnp.int32)
    for e in range(50):
        member = jnp.where((listed[:, e : e + 1] == lane) & (e < counts), 1, member)
    union = jnp.where(
        row < 4,
        jnp.max(member[0:4], axis=0, keepdims=True),
        jnp.max(member[4:8], axis=0, keepdims=True),
    )

    def ahead(a, n):
        return a if n == 0 else pltpu.roll(a, 128 - n, 1)

    us = [ahead(union, n) > 0 for n in range(4)]
    ms = [ahead(member, n) for n in range(4)]
    f0 = 2 * p * 8 + x * 2 + c
    near = jnp.abs((lane >> 2) - jnp.where(row < 4, f0, f0 + 8)) <= 1
    idx0 = jnp.where(us[0], 0, jnp.where(us[1], 1, jnp.where(us[2], 2, 3)))
    idx1 = jnp.where(us[3], 3, jnp.where(us[2], 2, jnp.where(us[1], 1, 0)))
    idx1 = jnp.where(idx1 == idx0, (idx0 + 1) & 3, idx1)
    idx0 = jnp.where(near, 0, idx0)
    idx1 = jnp.where(near, 1, idx1)

    def at(idx):
        return jnp.where(idx == 0, ms[0], jnp.where(idx == 1, ms[1], jnp.where(idx == 2, ms[2], ms[3])))

    tabv[0] = idx0
    tabv[1] = idx1
    tabv[2] = at(idx0)
    tabv[3] = at(idx1)
    tcopy = pltpu.make_async_copy(tabv, tabs, wsem.at[4])
    tcopy.start()
    tcopy.wait()
    l_copy(i).wait_send()
    c_copy(i).wait_send()

    for cp in wcopies[:3]:
        cp.wait()

    slot_own = p * 8 + x * 2 + c

    def head_norm(piece, gain):
        power = jnp.mean(piece * piece, axis=-1, keepdims=True)
        return piece * lax.rsqrt(power + EPS) * gain[...]

    def project(h):
        a = tok[h].reshape(256, D)
        for n in (1, 2):
            acc = jnp.dot(a, w[n], preferred_element_type=jnp.float32)
            for hd in range(2):
                piece = acc[:, hd * HD : (hd + 1) * HD]
                if n == 1:
                    piece = head_norm(piece, kg_ref)
                stkv[h, hd, n - 1] = piece.astype(jnp.bfloat16)
        s_kv(h, i).start()
        kv[slot_own, h, i] = stkv[h, i]
        acc = jnp.dot(a, w[0], preferred_element_type=jnp.float32)
        for hd in range(2):
            piece = head_norm(acc[:, hd * HD : (hd + 1) * HD], qg_ref)
            stq[h, hd] = jnp.transpose(piece).astype(jnp.bfloat16)
        s_q(h, i).start()
        qbuf[i, h] = stq[h, i]

    def s_kv(h, who):
        return rcopy(stkv.at[h, 1 - i], kv.at[slot_own, h, who], ssend.at[h, 0], srecv.at[h, 0], pair_dev)

    def s_q(h, who):
        return rcopy(stq.at[h, 1 - i], qbuf.at[who, h], ssend.at[h, 1], srecv.at[h, 1], pair_dev)

    def k_copy(h, ff, slot, e, dev):
        return rcopy(kv.at[slot, h, ff], kv.at[slot, h, ff], ksend.at[h, ff, e], krecv.at[h, ff, slot], dev)

    def swap_in(h):
        def send(ff):
            k_copy(h, ff, slot_own, 0, far_dev).start()
            k_copy(h, ff, slot_own, 1, xdev(1)).start()
            k_copy(h, ff, slot_own, 2, xdev(-1)).start()
            k_copy(h, ff, slot_own, 3, core_dev).start()

        send(i)
        s_kv(h, 1 - i).wait_recv()
        send(1 - i)
        s_q(h, 1 - i).wait_recv()

    t_own_in(1).wait_recv()
    t_fwd().start()
    t_anti(0).wait_recv()
    t_other(0, 1, y).start()
    t_other(0, -1, y).start()
    t_own_in(-1).wait_recv()
    t_fwd_in().wait_recv()
    project(0)
    t_anti(1).wait_recv()
    t_other(1, 1, y).start()
    t_other(1, -1, y).start()
    t_other(0, 1, yy(-d)).wait_recv()
    t_other_fwd(0, yy(-d)).start()
    swap_in(0)

    factor = (HD ** -0.5) * math.log2(math.e)
    lane1 = lax.broadcasted_iota(jnp.int32, (1, 128), 1)

    def attend(fi, h, parts):
        q = qbuf[fi, h]
        old = m[fi, h, 0:1]
        new = old
        tiles = []
        for keys, _, bias in parts:
            scores = jnp.dot(keys, q, preferred_element_type=jnp.float32) * factor
            if bias is not None:
                scores = (scores.reshape(4, 64, 256) + bias).reshape(256, 256)
            tiles.append(scores)
            new = jnp.maximum(new, jnp.max(scores, axis=0, keepdims=True))
        decay = jnp.exp2(old - new)
        total = l[fi, h, 0:1] * decay
        summed = o[fi, h] * decay
        for scores, (_, values, _) in zip(tiles, parts):
            weights = jnp.exp2(scores - new)
            total = total + jnp.sum(weights, axis=0, keepdims=True)
            summed = summed + jnp.dot(values, weights.astype(jnp.bfloat16), preferred_element_type=jnp.float32)
        m[fi, h, 0:1] = new
        l[fi, h, 0:1] = total
        o[fi, h] = summed

    def near_pass(n, carry):
        fi, df = n // 3, n % 3 - 1
        f = (2 * p + fi) * 8 + x * 2 + c + df

        @pl.when(jnp.logical_and(f >= 0, f <= 31))
        def _():
            fz = f // 8
            slot = (fz // 2) * 8 + f % 8
            keys = jnp.concatenate([kv[slot, h, fz % 2, 0, 128:256] for h in range(2)], axis=0)
            values = jnp.transpose(
                jnp.concatenate([kv[slot, h, fz % 2, 1, 128:256] for h in range(2)], axis=0)
            )
            for h in range(2):
                attend(fi, h, [(keys, values, None)])

        return carry

    def chosen(fi, base):
        rows, bias = [], []
        for ff in range(2):
            at4 = (base + 8 * ff) * 4
            rows.append([tabs[t, fi * 4, at4] for t in range(2)])
            for t in range(2):
                b = [jnp.where(tabs[2 + t, fi * 4 + e, at4] > 0, 0.0, LOW) for e in range(4)]
                across = [jnp.where(lane1 < 64, b[2 * e], b[2 * e + 1]) for e in range(2)]
                bias.append(jnp.concatenate(across, axis=1).reshape(1, 1, 256))
        bias = jnp.concatenate(bias, axis=0)

        def group(oc):
            keys, values = (
                jnp.concatenate([kvp[oc, ff, t, rows[ff][e]] for ff in range(2) for e in range(2)], axis=0)
                for t in range(2)
            )
            return keys, jnp.transpose(values), bias

        return group

    def slot_of(j, oc):
        dp = pick(j == 3, 1, pick(j >= 5, 1, 0))
        dxs = pick(j % 4 == 1, -1, pick(j == 2, 1, pick(j == 6, 1, pick(j == 4, 2, pick(j == 7, 2, 0)))))
        dd = d * (1 - 2 * oc)
        return ((p + dp) % 2) * 8 + ((x + dd * dxs + 8) % 4) * 2 + (c + oc) % 2

    def arrive(h, j):
        slot = slot_of(j, 0)
        for ff in range(2):

            @pl.when(j > 0)
            def _():
                k_copy(h, ff, slot, 0, core_dev).wait_recv()

            @pl.when(j % 4 == 1)
            def _():
                k_copy(h, ff, slot, 11 + j // 4, xdev(d)).start()

            @pl.when(j == 3)
            def _():
                k_copy(h, ff, slot, 13, xdev(1)).start()
                k_copy(h, ff, slot, 14, xdev(-1)).start()

            @pl.when(j > 0)
            def _():
                k_copy(h, ff, slot, 3 + j, core_dev).start()

    def arrive_other(h, j):
        for ff in range(2):
            k_copy(h, ff, slot_of(j, 1), 0, core_dev).wait_recv()

    def consume(h, j, halves):
        slots = [slot_of(j, oc) for oc in range(2)]
        for oc in range(2):
            kvp[oc] = kv[slots[oc], h].reshape(2, 2, 4, 64, HD)
        for fi in range(2):
            parts = [chosen(fi, (slot // 8) * 16 + slot % 8)(oc) for oc, slot in enumerate(slots)]
            for qh in halves:
                attend(fi, qh, parts)

    def phase0(j, carry):
        @pl.when(j == 1)
        def _():
            t_other(1, 1, yy(-d)).wait_recv()
            t_other_fwd(1, yy(-d)).start()

        @pl.when(j == 2)
        def _():
            for e in range(2):
                t_other(e, -1, yy(d)).wait_recv()
                t_other_fwd(e, yy(2)).wait_recv()
            project(1)

        @pl.when(j == 4)
        def _():
            swap_in(1)

        @pl.when(j == 7)
        def _():
            arrive(1, 1)

        arrive(0, j)

        @pl.when(j >= 4)
        def _():
            consume(0, j - 4, (1,))

        arrive_other(0, j)
        consume(0, j, (0,))
        return carry

    def phase1(j, carry):
        @pl.when(jnp.logical_and(j > 4, j < 7))
        def _():
            arrive(1, j - 3)

        consume(0, j, (1,))
        return carry

    def phase2(j, carry):
        @pl.when(jnp.logical_and(j >= 2, j <= 5))
        def _():
            arrive(1, j + 2)

        @pl.when(j == 7)
        def _():
            lax.fori_loop(0, 6, near_pass, 0)

        arrive_other(1, j)
        consume(1, j, (0, 1))
        return carry

    lax.fori_loop(0, 8, phase0, 0)
    lax.fori_loop(4, 8, phase1, 0)
    lax.fori_loop(0, 8, phase2, 0)

    def result(fi, h):
        return jnp.transpose(o[fi, h] / l[fi, h, 0:1]).astype(jnp.bfloat16)

    def a_copy(h, head):
        return rcopy(atts.at[h], attb.at[head, h], asend.at[h], arecv.at[h], pair_dev)

    for h in (1, 0):
        atts[h] = result(1 - i, h)
        a_copy(h, i).start()
    for h in (1, 0):
        attb[i, h] = result(i, h)
    wcopies[3].wait()

    def r_out(q, dest):
        return rcopy(part.at[q, dest], rfwd.at[q], rsend.at[q, 0], rrecv.at[q, 0], ydev(d))

    def r_a(q):
        return rcopy(part.at[q, yy(d)], ra.at[q], rsend.at[q, 1], rrecv.at[q, 1], ydev(d))

    def r_b(q):
        return rcopy(part.at[q, yy(-d)], rb.at[q], rsend.at[q, 2], rrecv.at[q, 2], ydev(-d))

    def r_z(cc):
        return rcopy(zsend.at[cc], rz.at[cc], rsend.at[NC + cc, 3], rrecv.at[NC + cc, 3], anti_dev)

    def out_project(h, cc, rows):
        q = NC * h + cc
        res = jnp.dot(rows, wo[:, cc * CW : (cc + 1) * CW], preferred_element_type=jnp.float32)
        part[q] = res.astype(jnp.bfloat16).reshape(4, 64, CW)

    def out_sends(first):
        for q in (first, first + 1):
            r_out(q, yy(2)).start()

    def chain(first):
        for q in (first, first + 1):
            r_out(q, yy(2)).wait_recv()
            part[q, yy(d)] = (part[q, yy(d)].astype(jnp.float32) + rfwd[q].astype(jnp.float32)).astype(jnp.bfloat16)
            r_a(q).start()
            r_b(q).start()

    def gathered(q):
        r_a(q).wait_recv()
        r_b(q).wait_recv()
        return part[q, y].astype(jnp.float32) + ra[q].astype(jnp.float32) + rb[q].astype(jnp.float32)

    def to_anti(first):
        for cc in (first, first + 1):
            zsend[cc] = gathered(NC + cc).astype(jnp.bfloat16)
            r_z(cc).start()

    for h in (1, 0):
        a_copy(h, 1 - i).wait_recv()
        rows = jnp.concatenate([attb[0, h], attb[1, h]], axis=1)
        for cc in range(NC):
            out_project(h, cc, rows)
            if h == 1 and cc == 1:
                out_sends(NC)
    out_sends(NC + 2)
    chain(NC)
    out_sends(0)
    chain(NC + 2)
    to_anti(0)
    out_sends(2)
    chain(0)
    to_anti(2)
    chain(2)
    for cc in range(NC):
        total = gathered(cc)
        r_z(cc).wait_recv()
        cols = slice(cc * CW, (cc + 1) * CW)
        out_ref[:, cols] = ((total + rz[cc].astype(jnp.float32)) * gate_ref[:, cols]).astype(jnp.bfloat16)

    for n in range(2):
        t_anti(n).wait_send()
        t_other(n, 1, y).wait_send()
        t_other(n, -1, y).wait_send()
        t_other_fwd(n, yy(-d)).wait_send()
    t_own(1).wait_send()
    t_own(-1).wait_send()
    t_fwd().wait_send()
    for h in range(2):
        s_kv(h, i).wait_send()
        s_q(h, i).wait_send()
        a_copy(h, i).wait_send()
        for ff in range(2):
            for e in range(15):
                k_copy(h, ff, slot_own, e, core_dev).wait_send()
    for q in range(2 * NC):
        r_out(q, yy(2)).wait_send()
        r_a(q).wait_send()
        r_b(q).wait_send()
    for cc in range(NC):
        r_z(cc).wait_send()


def body(tokens, mod_shift, mod_scale, mod_gate, w_query, w_key, w_value, q_gain, k_gain, w_out, kv_blocks, kv_count):
    vmem = pl.BlockSpec(memory_space=pltpu.VMEM)
    hbm = pl.BlockSpec(memory_space=pltpu.HBM)
    bf16, f32, i32 = jnp.bfloat16, jnp.float32, jnp.int32
    dma = pltpu.SemaphoreType.DMA
    return pl.pallas_call(
        kernel,
        out_shape=jax.ShapeDtypeStruct((64, D), bf16),
        in_specs=[hbm] * 12,
        out_specs=vmem,
        scratch_shapes=[
            pltpu.VMEM((64, D), bf16),
            pltpu.VMEM((1, D), f32),
            pltpu.VMEM((1, D), f32),
            pltpu.VMEM((1, D), f32),
            pltpu.VMEM((1, HD), f32),
            pltpu.VMEM((1, HD), f32),
            pltpu.VMEM((3, D, 256), bf16),
            pltpu.VMEM((256, D), bf16),
            pltpu.VMEM((2, 4, 64, D), bf16),
            pltpu.VMEM((2, 4, 50), i32),
            pltpu.VMEM((2, 1, 4), i32),
            pltpu.VMEM((4, 8, 128), i32),
            pltpu.SMEM((4, 8, 128), i32),
            pltpu.VMEM((2, 2, HD, 256), bf16),
            pltpu.VMEM((2, 2, 2, 256, HD), bf16),
            pltpu.VMEM((2, 2, HD, 256), bf16),
            pltpu.VMEM((16, 2, 2, 2, 256, HD), bf16),
            pltpu.VMEM((2, 2, 2, 4, 64, HD), bf16),
            pltpu.VMEM((2, 2, 8, 256), f32),
            pltpu.VMEM((2, 2, 8, 256), f32),
            pltpu.VMEM((2, 2, HD, 256), f32),
            pltpu.VMEM((2, 2, 256, HD), bf16),
            pltpu.VMEM((2, 256, HD), bf16),
            pltpu.VMEM((2 * NC, 4, 64, CW), bf16),
            pltpu.VMEM((2 * NC, 64, CW), bf16),
            pltpu.VMEM((2 * NC, 64, CW), bf16),
            pltpu.VMEM((2 * NC, 64, CW), bf16),
            pltpu.VMEM((NC, 64, CW), bf16),
            pltpu.VMEM((NC, 64, CW), bf16),
            dma((8,)),
            dma((5,)),
            dma((4,)),
            dma((11,)),
            dma((11,)),
            dma((2, 2)),
            dma((2, 2)),
            dma((2, 2, 15)),
            dma((2, 2, 16)),
            dma((2,)),
            dma((2,)),
            dma((2 * NC, 4)),
            dma((2 * NC, 4)),
        ],
        compiler_params=pltpu.CompilerParams(
            collective_id=0, has_side_effects=True, vmem_limit_bytes=56 * 2**20
        ),
        name="radial_block",
    )(
        tokens,
        mod_shift.reshape(1, D),
        mod_scale.reshape(1, D),
        mod_gate.reshape(1, D),
        w_query,
        w_key,
        w_value,
        q_gain.reshape(1, HD),
        k_gain.reshape(1, HD),
        w_out,
        kv_blocks,
        kv_count.reshape(1, 4),
    )


def solution(mesh):
    placed = (
        P(("seq", "uly"), None),
        P(),
        P(),
        P(),
        P(None, "uly"),
        P(None, "uly"),
        P(None, "uly"),
        P(),
        P(),
        P("uly", None),
        P("seq", None),
        P("seq"),
    )
    return jax.shard_map(
        body, mesh=mesh, in_specs=placed, out_specs=P(("seq", "uly"), None), check_vma=False
    )
```

```python
import functools
import math

import jax
import jax.numpy as jnp
from jax import lax
from jax.experimental import pallas as pl
from jax.experimental.pallas import tpu as pltpu
from jax.sharding import PartitionSpec as P

MESH = pl.DeviceIdType.MESH
EPS = 1e-06
D = 3072
HD = 128
LOW = -1e30
NC = 4
CW = D // NC


def pick(cond, a, b):
    return jnp.where(cond, a, b)


def kernel(
    tokens_in, shift_in, scale_in, gate_in, wq_ref, wk_ref, wv_ref, qg_in, kg_in, wo_ref, lists_in, counts_in,
    out_ref,
    tokens_ref, shift_ref, scale_ref, gate_ref, qg_ref, kg_ref,
    w, wo, tok, lst, cnt, tabv, tabs, stq, stkv, qbuf, kv, kvp, m, l, o, attb, atts, part, rfwd, ra, rb, rz, zsend,
    isem, wsem, lsem, tsend, trecv, ssend, srecv, ksend, krecv, asend, arecv, rsend, rrecv,
):
    s = lax.axis_index("seq")
    u = lax.axis_index("uly")
    zl, x, c = s // 8, (s // 2) % 4, s % 2
    i, p = zl % 2, zl // 2
    y, zh = u // 2, u % 2
    d = 1 - 2 * c

    def xdev(e):
        return (zl * 8 + ((x + e + 8) % 4) * 2 + c, u)

    def yy(e):
        return (y + e + 8) % 4

    def ydev(e):
        return (s, yy(e) * 2 + zh)

    core_dev = (s + 1 - 2 * c, u)
    pair_dev = (s + 8 * (1 - 2 * i), u)
    far_dev = (s + 16 * (1 - 2 * p), u)
    anti_dev = (s, y * 2 + 1 - zh)

    def rcopy(src, dst, ss, rs, dev):
        return pltpu.make_async_remote_copy(
            src_ref=src, dst_ref=dst, send_sem=ss, recv_sem=rs, device_id=dev, device_id_type=MESH
        )

    icopies = [
        pltpu.make_async_copy(src, dst, isem.at[n])
        for n, (src, dst) in enumerate(
            (
                (tokens_in, tokens_ref),
                (scale_in, scale_ref),
                (shift_in, shift_ref),
                (lists_in, lst.at[i]),
                (counts_in, cnt.at[i]),
                (qg_in, qg_ref),
                (kg_in, kg_ref),
                (gate_in, gate_ref),
            )
        )
    ]
    wcopies = [pltpu.make_async_copy(r, w.at[n], wsem.at[n]) for n, r in enumerate((wq_ref, wk_ref, wv_ref))]
    wcopies.append(pltpu.make_async_copy(wo_ref, wo, wsem.at[3]))
    for cp in icopies + wcopies:
        cp.start()

    barrier = pltpu.get_barrier_semaphore()
    for dev in (core_dev, pair_dev, far_dev, anti_dev, xdev(1), xdev(-1), ydev(1), ydev(-1)):
        pl.semaphore_signal(barrier, inc=1, device_id=dev, device_id_type=MESH)

    for cp in icopies:
        cp.wait()
    vals = tokens_ref[...].astype(jnp.float32)
    center = jnp.mean(vals, axis=-1, keepdims=True)
    vals = vals - center
    spread = jnp.mean(vals * vals, axis=-1, keepdims=True)
    vals = vals * lax.rsqrt(spread + EPS)
    tok[0, y] = (vals * (1.0 + scale_ref[...]) + shift_ref[...]).astype(jnp.bfloat16)

    pl.semaphore_wait(barrier, 8)

    def half_rows(n):
        return pl.ds(32 * n, 32)

    def t_anti(n):
        return rcopy(tok.at[0, y, half_rows(n)], tok.at[1, y, half_rows(n)], tsend.at[n], trecv.at[n], anti_dev)

    def t_own(e):
        k = 2 if e == 1 else 3
        return rcopy(tok.at[0, y], tok.at[0, y], tsend.at[k], trecv.at[k], ydev(d * e))

    def t_own_in(e):
        k = 2 if e == 1 else 3
        sl = yy(-d * e)
        return rcopy(tok.at[0, sl], tok.at[0, sl], tsend.at[k], trecv.at[k], ydev(d * e))

    def t_fwd():
        sl = yy(-d)
        return rcopy(tok.at[0, sl], tok.at[0, sl], tsend.at[4], trecv.at[4], ydev(d))

    def t_fwd_in():
        sl = yy(2)
        return rcopy(tok.at[0, sl], tok.at[0, sl], tsend.at[4], trecv.at[4], ydev(d))

    def t_other(n, e, sl):
        k = 5 + 2 * n + (0 if e == 1 else 1)
        return rcopy(tok.at[1, sl, half_rows(n)], tok.at[1, sl, half_rows(n)], tsend.at[k], trecv.at[k], ydev(d * e))

    def t_other_fwd(n, sl):
        k = 9 + n
        return rcopy(tok.at[1, sl, half_rows(n)], tok.at[1, sl, half_rows(n)], tsend.at[k], trecv.at[k], ydev(d))

    def l_copy(row):
        return rcopy(lst.at[row], lst.at[row], lsem.at[0], lsem.at[1], pair_dev)

    def c_copy(row):
        return rcopy(cnt.at[row], cnt.at[row], lsem.at[2], lsem.at[3], pair_dev)

    l_copy(i).start()
    c_copy(i).start()
    t_anti(0).start()
    t_own(1).start()
    t_own(-1).start()
    t_anti(1).start()

    m[...] = jnp.full(m.shape, LOW, jnp.float32)
    l[...] = jnp.zeros(l.shape, jnp.float32)
    o[...] = jnp.zeros(o.shape, jnp.float32)
    l_copy(1 - i).wait_recv()
    c_copy(1 - i).wait_recv()
    listed = jnp.concatenate([lst[0], lst[1]], axis=0)
    lane = lax.broadcasted_iota(jnp.int32, (8, 128), 1)
    row = lax.broadcasted_iota(jnp.int32, (8, 128), 0)
    counts = jnp.zeros((8, 128), jnp.int32)
    for e in range(8):
        counts = jnp.where(row == e, cnt[e // 4][:, e % 4 : e % 4 + 1], counts)
    member = jnp.zeros((8, 128), jnp.int32)
    for e in range(50):
        member = jnp.where((listed[:, e : e + 1] == lane) & (e < counts), 1, member)
    union = jnp.where(
        row < 4,
        jnp.max(member[0:4], axis=0, keepdims=True),
        jnp.max(member[4:8], axis=0, keepdims=True),
    )

    def ahead(a, n):
        return a if n == 0 else pltpu.roll(a, 128 - n, 1)

    us = [ahead(union, n) > 0 for n in range(4)]
    ms = [ahead(member, n) for n in range(4)]
    f0 = 2 * p * 8 + x * 2 + c
    near = jnp.abs((lane >> 2) - jnp.where(row < 4, f0, f0 + 8)) <= 1
    idx0 = jnp.where(us[0], 0, jnp.where(us[1], 1, jnp.where(us[2], 2, 3)))
    idx1 = jnp.where(us[3], 3, jnp.where(us[2], 2, jnp.where(us[1], 1, 0)))
    idx1 = jnp.where(idx1 == idx0, (idx0 + 1) & 3, idx1)
    idx0 = jnp.where(near, 0, idx0)
    idx1 = jnp.where(near, 1, idx1)

    def at(idx):
        return jnp.where(idx == 0, ms[0], jnp.where(idx == 1, ms[1], jnp.where(idx == 2, ms[2], ms[3])))

    tabv[0] = idx0
    tabv[1] = idx1
    tabv[2] = at(idx0)
    tabv[3] = at(idx1)
    tcopy = pltpu.make_async_copy(tabv, tabs, wsem.at[4])
    tcopy.start()
    tcopy.wait()
    l_copy(i).wait_send()
    c_copy(i).wait_send()

    for cp in wcopies[:3]:
        cp.wait()

    slot_own = p * 8 + x * 2 + c

    def head_norm(piece, gain):
        power = jnp.mean(piece * piece, axis=-1, keepdims=True)
        return piece * lax.rsqrt(power + EPS) * gain[...]

    def project(h):
        a = tok[h].reshape(256, D)
        for n in (1, 2):
            acc = jnp.dot(a, w[n], preferred_element_type=jnp.float32)
            for hd in range(2):
                piece = acc[:, hd * HD : (hd + 1) * HD]
                if n == 1:
                    piece = head_norm(piece, kg_ref)
                stkv[h, hd, n - 1] = piece.astype(jnp.bfloat16)
        s_kv(h, i).start()
        kv[slot_own, h, i] = stkv[h, i]
        acc = jnp.dot(a, w[0], preferred_element_type=jnp.float32)
        for hd in range(2):
            piece = head_norm(acc[:, hd * HD : (hd + 1) * HD], qg_ref)
            stq[h, hd] = jnp.transpose(piece).astype(jnp.bfloat16)
        s_q(h, i).start()
        qbuf[i, h] = stq[h, i]

    def s_kv(h, who):
        return rcopy(stkv.at[h, 1 - i], kv.at[slot_own, h, who], ssend.at[h, 0], srecv.at[h, 0], pair_dev)

    def s_q(h, who):
        return rcopy(stq.at[h, 1 - i], qbuf.at[who, h], ssend.at[h, 1], srecv.at[h, 1], pair_dev)

    def k_copy(h, ff, slot, e, dev):
        return rcopy(kv.at[slot, h, ff], kv.at[slot, h, ff], ksend.at[h, ff, e], krecv.at[h, ff, slot], dev)

    def swap_in(h):
        def send(ff):
            k_copy(h, ff, slot_own, 0, far_dev).start()
            k_copy(h, ff, slot_own, 1, xdev(1)).start()
            k_copy(h, ff, slot_own, 2, xdev(-1)).start()
            k_copy(h, ff, slot_own, 3, core_dev).start()

        send(i)
        s_kv(h, 1 - i).wait_recv()
        send(1 - i)
        s_q(h, 1 - i).wait_recv()

    t_own_in(1).wait_recv()
    t_fwd().start()
    t_anti(0).wait_recv()
    t_other(0, 1, y).start()
    t_other(0, -1, y).start()
    t_own_in(-1).wait_recv()
    t_fwd_in().wait_recv()
    project(0)
    t_anti(1).wait_recv()
    t_other(1, 1, y).start()
    t_other(1, -1, y).start()
    t_other(0, 1, yy(-d)).wait_recv()
    t_other_fwd(0, yy(-d)).start()
    swap_in(0)

    factor = (HD ** -0.5) * math.log2(math.e)
    lane1 = lax.broadcasted_iota(jnp.int32, (1, 128), 1)

    def attend(fi, h, parts):
        q = qbuf[fi, h]
        old = m[fi, h, 0:1]
        new = old
        tiles = []
        for keys, _, bias in parts:
            scores = jnp.dot(keys, q, preferred_element_type=jnp.float32) * factor
            if bias is not None:
                scores = (scores.reshape(bias.shape[0], -1, 256) + bias).reshape(scores.shape)
            tiles.append(scores)
            new = jnp.maximum(new, jnp.max(scores, axis=0, keepdims=True))
        decay = jnp.exp2(old - new)
        total = l[fi, h, 0:1] * decay
        summed = o[fi, h] * decay
        for scores, (_, values, _) in zip(tiles, parts):
            weights = jnp.exp2(scores - new)
            total = total + jnp.sum(weights, axis=0, keepdims=True)
            summed = summed + jnp.dot(values, weights.astype(jnp.bfloat16), preferred_element_type=jnp.float32)
        m[fi, h, 0:1] = new
        l[fi, h, 0:1] = total
        o[fi, h] = summed

    def near(half, fi):
        keys, values, bias = [], [], []
        for df in (-1, 0, 1):
            f = (2 * p + fi) * 8 + x * 2 + c + df
            inside = jnp.logical_and(f >= 0, f <= 31)
            f = (f + 32) % 32
            fz = f // 8
            slot = (fz // 2) * 8 + f % 8
            keys.append(kv[slot, half, fz % 2, 0, 128:256])
            values.append(kv[slot, half, fz % 2, 1, 128:256])
            bias.append(jnp.broadcast_to(jnp.where(inside, 0.0, LOW), (1, 128, 256)))
        keys = jnp.concatenate(keys, axis=0)
        values = jnp.transpose(jnp.concatenate(values, axis=0))
        bias = jnp.concatenate(bias, axis=0)
        for h in range(2):
            attend(fi, h, [(keys, values, bias)])

    def chosen(fi, base):
        rows, bias = [], []
        for ff in range(2):
            at4 = (base + 8 * ff) * 4
            rows.append([tabs[t, fi * 4, at4] for t in range(2)])
            for t in range(2):
                b = [jnp.where(tabs[2 + t, fi * 4 + e, at4] > 0, 0.0, LOW) for e in range(4)]
                across = [jnp.where(lane1 < 64, b[2 * e], b[2 * e + 1]) for e in range(2)]
                bias.append(jnp.concatenate(across, axis=1).reshape(1, 1, 256))
        bias = jnp.concatenate(bias, axis=0)

        def group(oc):
            keys, values = (
                jnp.concatenate([kvp[oc, ff, t, rows[ff][e]] for ff in range(2) for e in range(2)], axis=0)
                for t in range(2)
            )
            return keys, jnp.transpose(values), bias

        return group

    def slot_of(j, oc):
        dp = pick(j == 3, 1, pick(j >= 5, 1, 0))
        dxs = pick(j % 4 == 1, -1, pick(j == 2, 1, pick(j == 6, 1, pick(j == 4, 2, pick(j == 7, 2, 0)))))
        dd = d * (1 - 2 * oc)
        return ((p + dp) % 2) * 8 + ((x + dd * dxs + 8) % 4) * 2 + (c + oc) % 2

    def arrive(h, j):
        slot = slot_of(j, 0)
        for ff in range(2):

            @pl.when(j > 0)
            def _():
                k_copy(h, ff, slot, 0, core_dev).wait_recv()

            @pl.when(j % 4 == 1)
            def _():
                k_copy(h, ff, slot, 11 + j // 4, xdev(d)).start()

            @pl.when(j == 3)
            def _():
                k_copy(h, ff, slot, 13, xdev(1)).start()
                k_copy(h, ff, slot, 14, xdev(-1)).start()

            @pl.when(j > 0)
            def _():
                k_copy(h, ff, slot, 3 + j, core_dev).start()

    def arrive_other(h, j):
        for ff in range(2):
            k_copy(h, ff, slot_of(j, 1), 0, core_dev).wait_recv()

    def consume(h, j, halves):
        slots = [slot_of(j, oc) for oc in range(2)]
        for oc in range(2):
            kvp[oc] = kv[slots[oc], h].reshape(2, 2, 4, 64, HD)
        for fi in range(2):
            parts = [chosen(fi, (slot // 8) * 16 + slot % 8)(oc) for oc, slot in enumerate(slots)]
            for qh in halves:
                attend(fi, qh, parts)

    def phase0(j, carry):
        @pl.when(j == 0)
        def _():
            t_other(1, 1, yy(-d)).wait_recv()
            t_other_fwd(1, yy(-d)).start()

        @pl.when(j == 2)
        def _():
            for e in range(2):
                t_other(e, -1, yy(d)).wait_recv()
                t_other_fwd(e, yy(2)).wait_recv()
            project(1)

        @pl.when(j == 4)
        def _():
            swap_in(1)

        @pl.when(j == 7)
        def _():
            arrive(1, 1)

        arrive(0, j)

        @pl.when(j >= 4)
        def _():
            consume(0, j - 4, (1,))

        arrive_other(0, j)
        consume(0, j, (0,))
        return carry

    def phase1(j, carry):
        @pl.when(jnp.logical_and(j > 4, j < 7))
        def _():
            arrive(1, j - 3)

        consume(0, j, (1,))

        @pl.when(j == 7)
        def _():
            near(0, 0)
            near(0, 1)

        return carry

    def phase2(j, carry):
        @pl.when(jnp.logical_or(j == 2, j == 3))
        def _():
            arrive(1, j + 2)

        @pl.when(j == 7)
        def _():
            near(1, 0)
            near(1, 1)

        arrive_other(1, j)
        consume(1, j, (0, 1))

        @pl.when(jnp.logical_or(j == 4, j == 5))
        def _():
            arrive(1, j + 2)

        return carry

    lax.fori_loop(0, 8, phase0, 0)
    lax.fori_loop(4, 8, phase1, 0)
    lax.fori_loop(0, 8, phase2, 0)

    def result(fi, h):
        return jnp.transpose(o[fi, h] / l[fi, h, 0:1]).astype(jnp.bfloat16)

    def a_copy(h, head):
        return rcopy(atts.at[h], attb.at[head, h], asend.at[h], arecv.at[h], pair_dev)

    for h in (1, 0):
        atts[h] = result(1 - i, h)
        a_copy(h, i).start()
    for h in (1, 0):
        attb[i, h] = result(i, h)
    wcopies[3].wait()

    def r_out(q, dest):
        return rcopy(part.at[q, dest], rfwd.at[q], rsend.at[q, 0], rrecv.at[q, 0], ydev(d))

    def r_a(q):
        return rcopy(part.at[q, yy(d)], ra.at[q], rsend.at[q, 1], rrecv.at[q, 1], ydev(d))

    def r_b(q):
        return rcopy(part.at[q, yy(-d)], rb.at[q], rsend.at[q, 2], rrecv.at[q, 2], ydev(-d))

    def r_z(cc):
        return rcopy(zsend.at[cc], rz.at[cc], rsend.at[NC + cc, 3], rrecv.at[NC + cc, 3], anti_dev)

    def out_project(h, cc, rows):
        q = NC * h + cc
        res = jnp.dot(rows, wo[:, cc * CW : (cc + 1) * CW], preferred_element_type=jnp.float32)
        part[q] = res.astype(jnp.bfloat16).reshape(4, 64, CW)

    def out_sends(first):
        for q in (first, first + 1):
            r_out(q, yy(2)).start()

    def chain(first):
        for q in (first, first + 1):
            r_out(q, yy(2)).wait_recv()
            part[q, yy(d)] = (part[q, yy(d)].astype(jnp.float32) + rfwd[q].astype(jnp.float32)).astype(jnp.bfloat16)
            r_a(q).start()
            r_b(q).start()

    def gathered(q):
        r_a(q).wait_recv()
        r_b(q).wait_recv()
        return part[q, y].astype(jnp.float32) + ra[q].astype(jnp.float32) + rb[q].astype(jnp.float32)

    def to_anti(first):
        for cc in (first, first + 1):
            zsend[cc] = gathered(NC + cc).astype(jnp.bfloat16)
            r_z(cc).start()

    for h in (1, 0):
        a_copy(h, 1 - i).wait_recv()
        rows = jnp.concatenate([attb[0, h], attb[1, h]], axis=1)
        for cc in range(NC):
            out_project(h, cc, rows)
            if h == 1 and cc == 1:
                out_sends(NC)
    out_sends(NC + 2)
    chain(NC)
    out_sends(0)
    chain(NC + 2)
    to_anti(0)
    out_sends(2)
    chain(0)
    to_anti(2)
    chain(2)
    for cc in range(NC):
        total = gathered(cc)
        r_z(cc).wait_recv()
        cols = slice(cc * CW, (cc + 1) * CW)
        out_ref[:, cols] = ((total + rz[cc].astype(jnp.float32)) * gate_ref[:, cols]).astype(jnp.bfloat16)

    for n in range(2):
        t_anti(n).wait_send()
        t_other(n, 1, y).wait_send()
        t_other(n, -1, y).wait_send()
        t_other_fwd(n, yy(-d)).wait_send()
    t_own(1).wait_send()
    t_own(-1).wait_send()
    t_fwd().wait_send()
    for h in range(2):
        s_kv(h, i).wait_send()
        s_q(h, i).wait_send()
        a_copy(h, i).wait_send()
        for ff in range(2):
            for e in range(15):
                k_copy(h, ff, slot_own, e, core_dev).wait_send()
    for q in range(2 * NC):
        r_out(q, yy(2)).wait_send()
        r_a(q).wait_send()
        r_b(q).wait_send()
    for cc in range(NC):
        r_z(cc).wait_send()


def body(tokens, mod_shift, mod_scale, mod_gate, w_query, w_key, w_value, q_gain, k_gain, w_out, kv_blocks, kv_count):
    vmem = pl.BlockSpec(memory_space=pltpu.VMEM)
    hbm = pl.BlockSpec(memory_space=pltpu.HBM)
    bf16, f32, i32 = jnp.bfloat16, jnp.float32, jnp.int32
    dma = pltpu.SemaphoreType.DMA
    return pl.pallas_call(
        kernel,
        out_shape=jax.ShapeDtypeStruct((64, D), bf16),
        in_specs=[hbm] * 12,
        out_specs=vmem,
        scratch_shapes=[
            pltpu.VMEM((64, D), bf16),
            pltpu.VMEM((1, D), f32),
            pltpu.VMEM((1, D), f32),
            pltpu.VMEM((1, D), f32),
            pltpu.VMEM((1, HD), f32),
            pltpu.VMEM((1, HD), f32),
            pltpu.VMEM((3, D, 256), bf16),
            pltpu.VMEM((256, D), bf16),
            pltpu.VMEM((2, 4, 64, D), bf16),
            pltpu.VMEM((2, 4, 50), i32),
            pltpu.VMEM((2, 1, 4), i32),
            pltpu.VMEM((4, 8, 128), i32),
            pltpu.SMEM((4, 8, 128), i32),
            pltpu.VMEM((2, 2, HD, 256), bf16),
            pltpu.VMEM((2, 2, 2, 256, HD), bf16),
            pltpu.VMEM((2, 2, HD, 256), bf16),
            pltpu.VMEM((16, 2, 2, 2, 256, HD), bf16),
            pltpu.VMEM((2, 2, 2, 4, 64, HD), bf16),
            pltpu.VMEM((2, 2, 8, 256), f32),
            pltpu.VMEM((2, 2, 8, 256), f32),
            pltpu.VMEM((2, 2, HD, 256), f32),
            pltpu.VMEM((2, 2, 256, HD), bf16),
            pltpu.VMEM((2, 256, HD), bf16),
            pltpu.VMEM((2 * NC, 4, 64, CW), bf16),
            pltpu.VMEM((2 * NC, 64, CW), bf16),
            pltpu.VMEM((2 * NC, 64, CW), bf16),
            pltpu.VMEM((2 * NC, 64, CW), bf16),
            pltpu.VMEM((NC, 64, CW), bf16),
            pltpu.VMEM((NC, 64, CW), bf16),
            dma((8,)),
            dma((5,)),
            dma((4,)),
            dma((11,)),
            dma((11,)),
            dma((2, 2)),
            dma((2, 2)),
            dma((2, 2, 15)),
            dma((2, 2, 16)),
            dma((2,)),
            dma((2,)),
            dma((2 * NC, 4)),
            dma((2 * NC, 4)),
        ],
        compiler_params=pltpu.CompilerParams(
            collective_id=0, has_side_effects=True, vmem_limit_bytes=56 * 2**20
        ),
        name="radial_block",
    )(
        tokens,
        mod_shift.reshape(1, D),
        mod_scale.reshape(1, D),
        mod_gate.reshape(1, D),
        w_query,
        w_key,
        w_value,
        q_gain.reshape(1, HD),
        k_gain.reshape(1, HD),
        w_out,
        kv_blocks,
        kv_count.reshape(1, 4),
    )


def solution(mesh):
    placed = (
        P(("seq", "uly"), None),
        P(),
        P(),
        P(),
        P(None, "uly"),
        P(None, "uly"),
        P(None, "uly"),
        P(),
        P(),
        P("uly", None),
        P("seq", None),
        P("seq"),
    )
    return jax.shard_map(
        body, mesh=mesh, in_specs=placed, out_specs=P(("seq", "uly"), None), check_vma=False
    )
```
